256 devices in a mesh: seq: 16 (over x, z_lo, core), basis: 16 (over z_hi, y).
Axes of the slice: x: 4, y: 4, z: 8 (z_hi: 4, z_lo: 2; z = z_hi * 2 + z_lo), core: 2. Of those that a mesh axis runs over, the one named last changes fastest.
Arguments:
- up_input: bfloat16 [2048, 5120], P('seq'), may hold values from -6 to 6
- up_grad: bfloat16 [2048, 10240], P('seq', 'basis'), may hold values from -6 to 6
- down_input: bfloat16 [2048, 10240], P('seq', 'basis'), may hold values from -6 to 6
- down_grad: bfloat16 [2048, 5120], P('seq'), may hold values from -6 to 6
- width_up: bfloat16 [5120, 5120], P('basis', 'seq'), may hold values from -0.078125 to 0.078125
- width_down: bfloat16 [5120, 5120], P('basis', 'seq'), may hold values from -0.078125 to 0.078125
- hidden_up: bfloat16 [10240, 10240], P('seq', 'basis'), may hold values from -0.0625 to 0.0625
- hidden_down: bfloat16 [10240, 10240], P('seq', 'basis'), may hold values from -0.0625 to 0.0625
- query_up: bfloat16 [6, 10240, 5120], P(None, 'seq', 'basis'), may hold values from -0.0004272461 to 0.0004272461
- query_down: bfloat16 [6, 10240, 5120], P(None, 'seq', 'basis'), may hold values from -0.0004272461 to 0.0004272461
- eigen_up: float32 [10240, 5120], P('seq', 'basis'), may hold values from 0.05 to 20
- eigen_down: float32 [10240, 5120], P('seq', 'basis'), may hold values from 0.05 to 20
Outputs:
- token_scores: float32 [6, 2048], P(None, 'seq')
The draws below stay inside these ranges and needn't reach their ends.
All inputs are finite; a program needn't handle non-finite values.
Results may differ from the reference program's by a relative error of at most 0.025.
Values may be sent and summed in bfloat16 or wider, within the bound.
A program may use at most 128 MiB of HBM per device.

```python
import math
import jax
import jax.numpy as jnp
from jax import lax

D = 5120
F = 10240
NQ = 6
TOKENS = 2048
N_SEQ = 16
N_BASIS = 16


def steps_of(key, shape, split, least, largest):
    def one(position, blocks):
        heights = jax.random.uniform(jax.random.fold_in(jax.random.fold_in(key, 6), position), (blocks,), jnp.float32, least / len(split), largest / len(split))
        return jnp.repeat(jnp.exp(heights), shape[position] // blocks).reshape((-1,) + (1,) * (len(shape) - position - 1))

    factor_of = one(*split[0])
    for cut in split[1:]:
        factor_of = factor_of * one(*cut)
    return factor_of


def scatter_about(rng, dims, scale, bound, shards=(), dtype=jnp.bfloat16):
    array = jax.random.normal(rng, dims, jnp.float32) * scale
    if len(shards) > 0:
        array = steps_of(rng, dims, shards, -0.22, 0.18) * array
    return jnp.clip(array, min=-bound, max=bound).astype(dtype)


def setup_inputs(seed: int = 0) -> dict:
    keys = jax.random.split(jax.random.key(seed), 13)
    up_input = scatter_about(keys[0], (TOKENS, D), 1.0, 6.0, ((0, 16),))
    up_grad = scatter_about(keys[1], (TOKENS, F), 1.0, 6.0, ((0, 16), (1, 16)))
    down_input = scatter_about(keys[2], (TOKENS, F), 1.0, 6.0, ((0, 16), (1, 16)))
    down_grad = scatter_about(keys[3], (TOKENS, D), 1.0, 6.0, ((0, 16),))
    width_up = scatter_about(keys[4], (D, D), D ** -0.5, 0.078125, ((0, 16), (1, 16)))
    width_down = scatter_about(keys[5], (D, D), D ** -0.5, 0.078125, ((0, 16), (1, 16)))
    hidden_up = scatter_about(keys[6], (F, F), F ** -0.5, 0.0625, ((0, 16), (1, 16)))
    hidden_down = scatter_about(keys[7], (F, F), F ** -0.5, 0.0625, ((0, 16), (1, 16)))
    query_up = scatter_about(keys[8], (NQ, F, D), (4 * F * D) ** -0.5, 0.0004272461, ((1, 16), (2, 16)))
    query_down = scatter_about(keys[9], (NQ, F, D), (4 * F * D) ** -0.5, 0.0004272461, ((1, 16), (2, 16)))
    eigen_up = jnp.clip(jnp.exp(math.log(20.0) - 5.9914645 * jax.random.uniform(keys[10], (F, D), jnp.float32) ** steps_of(keys[10], (F, D), ((0, 16), (1, 16)), -0.2, 0.2)), 0.05, 20.0)
    eigen_down = jnp.clip(jnp.exp(math.log(20.0) - 5.9914645 * jax.random.uniform(keys[11], (F, D), jnp.float32) ** steps_of(keys[11], (F, D), ((0, 16), (1, 16)), -0.2, 0.2)), 0.05, 20.0)
    return dict(up_input=up_input, up_grad=up_grad, down_input=down_input, down_grad=down_grad, width_up=width_up, width_down=width_down, hidden_up=hidden_up, hidden_down=hidden_down, query_up=query_up, query_down=query_down, eigen_up=eigen_up, eigen_down=eigen_down)


DAMPING = 0.1


def settle(values):
    return lax.optimization_barrier(values.astype(jnp.bfloat16)).astype(jnp.float32)


def rotated(inputs, vectors, blocks):
    feature_width = inputs.shape[1] // blocks
    accumulated = jnp.zeros((inputs.shape[0], vectors.shape[0]), jnp.float32)
    for number in range(blocks):
        segment = inputs[:, number * feature_width:(number + 1) * feature_width]
        columns = vectors[:, number * feature_width:(number + 1) * feature_width]
        product = jnp.dot(segment, columns.T, preferred_element_type=jnp.float32)
        accumulated = accumulated + settle(product)
    return accumulated.astype(jnp.bfloat16)


def scores(hidden_side, width_side, queries, eigenvalues):
    hidden_wide = hidden_side.astype(jnp.float32)

    def single(query_one):
        weights = (query_one.astype(jnp.float32) / (eigenvalues + DAMPING)).astype(jnp.bfloat16)
        spread = jnp.dot(width_side, weights.T, preferred_element_type=jnp.float32)
        return jnp.sum(spread * hidden_wide, axis=1)

    return lax.map(single, queries)


def reference(up_input, up_grad, down_input, down_grad, width_up, width_down, hidden_up, hidden_down, query_up, query_down, eigen_up, eigen_down):
    hidden_upward = rotated(up_grad, hidden_up, N_BASIS)
    hidden_downward = rotated(down_input, hidden_down, N_BASIS)
    width_upward = rotated(up_input, width_up, N_SEQ)
    width_downward = rotated(down_grad, width_down, N_SEQ)
    upward = scores(hidden_upward, width_upward, query_up, eigen_up)
    downward = scores(hidden_downward, width_downward, query_down, eigen_down)
    return upward + downward
```

```python
import functools

import jax
import jax.numpy as jnp
from jax import lax
from jax.experimental import pallas as pl
from jax.experimental.pallas import tpu as pltpu
from jax.sharding import PartitionSpec as P

DAMPING = 0.1
MESH = pl.DeviceIdType.MESH
F32 = jnp.float32
BF16 = jnp.bfloat16

GROUPS = 8
ITERATIONS = 16


def dot_nt(a, b):
    return lax.dot_general(a, b, (((1,), (1,)), ((), ())), preferred_element_type=F32)


def kernel(
    up_input, up_grad, down_input, down_grad, width_up, width_down, hidden_up, hidden_down,
    query_up, query_down, eigen_up, eigen_down,
    out,
    xg, vh, part, r1, r2, r3, hid, vw, feat, wacc, wg, query, eigen, mult,
    acc, red_c, red_zl, red_x, red_y, red_zh, sum_x, sum_y,
    local_sem, x_send, x_recv, v_send, v_recv, w_send, w_recv,
    h_send, h_recv, red_send, red_recv,
):
    s = lax.axis_index("seq")
    b = lax.axis_index("basis")
    x, zl, c = s // 4, lax.rem(s // 2, 2), lax.rem(s, 2)
    zh, y = b // 4, lax.rem(b, 4)
    x1, x2, x3 = lax.rem(x + 1, 4), lax.rem(x + 2, 4), lax.rem(x + 3, 4)
    y1, y2, y3 = lax.rem(y + 1, 4), lax.rem(y + 2, 4), lax.rem(y + 3, 4)

    def slot(px, pzl, pc):
        return px * 4 + pzl * 2 + pc

    def at_y(py):
        return (s, zh * 4 + py)

    def at_zh(d):
        return (s, lax.rem(zh + d, 4) * 4 + y)

    def at_x(px):
        return (slot(px, zl, c), b)

    to_core = (slot(x, zl, 1 - c), b)
    to_zl = (slot(x, 1 - zl, c), b)

    def remote(src, dst, send, recv, to):
        return pltpu.make_async_remote_copy(
            src_ref=src, dst_ref=dst, send_sem=send, recv_sem=recv, device_id=to, device_id_type=MESH
        )

    moves = [
        (up_grad, xg.at[s, 0]),
        (down_input, xg.at[s, 1]),
        (hidden_up, vh.at[0]),
        (hidden_down, vh.at[1]),
        (width_up, vw.at[s, 0]),
        (width_down, vw.at[s, 1]),
        (query_up, query.at[0]),
        (query_down, query.at[1]),
        (eigen_up, eigen.at[0]),
        (eigen_down, eigen.at[1]),
        (up_input, feat.at[0]),
        (down_grad, feat.at[1]),
    ]
    loads = [pltpu.make_async_copy(a, d, local_sem.at[n]) for n, (a, d) in enumerate(moves)]
    for load in loads:
        load.start()

    barrier = pltpu.get_barrier_semaphore()
    partners = [to_core, to_zl, at_x(x1), at_x(x2), at_x(x3), at_y(y1), at_y(y2), at_y(y3)]
    partners += [at_zh(d) for d in (1, 2, 3)]
    for partner in partners:
        pl.semaphore_signal(barrier, inc=1, device_id=partner, device_id_type=MESH)
    pl.semaphore_wait(barrier, len(partners))

    def place(k):
        px = jnp.where(k < 2, x, jnp.where(k >= 6, x2, jnp.where(lax.rem(k, 2) == 0, x3, x1)))
        high = jnp.where((k == 3) | (k == 4) | (k == 7), 1, 0)
        pzl = jnp.where(k == 0, zl, jnp.where(k == 1, 1 - zl, high))
        return px * 4 + pzl * 2

    def gather_copy(buf, send, recv, k, way, to):
        block = buf.at[place(k) + c]
        return remote(block, block, send.at[way, k], recv.at[place(k) + c], to)

    def gather_send(buf, send, recv, k):
        gather_copy(buf, send, recv, k, 0, to_core).start()

        @pl.when(k == 0)
        def _():
            gather_copy(buf, send, recv, k, 1, to_zl).start()

        @pl.when(k <= 2)
        def _():
            gather_copy(buf, send, recv, k, 2, at_x(x1)).start()

        @pl.when((k <= 1) | (k == 3))
        def _():
            gather_copy(buf, send, recv, k, 3, at_x(x3)).start()

    def gather_wait(buf, send, recv, k):
        gather_copy(buf, send, recv, k, 0, to_core).wait_recv()

    def gather_wait_core(buf, send, recv, k):
        block = buf.at[place(k) + 1 - c]
        remote(block, block, send.at[0, k], recv.at[place(k) + 1 - c], to_core).wait_recv()

    def gather_step(buf, send, recv, k):
        @pl.when(k > 0)
        def _():
            gather_wait(buf, send, recv, k)

        gather_send(buf, send, recv, k)

    def gather_drain(buf, send, recv):
        def body(k, _):
            gather_copy(buf, send, recv, k, 0, to_core).wait_send()

            @pl.when(k == 0)
            def _():
                gather_copy(buf, send, recv, k, 1, to_zl).wait_send()

            @pl.when(k <= 2)
            def _():
                gather_copy(buf, send, recv, k, 2, at_x(x1)).wait_send()

            @pl.when((k <= 1) | (k == 3))
            def _():
                gather_copy(buf, send, recv, k, 3, at_x(x3)).wait_send()

            return 0

        lax.fori_loop(0, GROUPS, body, 0)

    x_gather = (xg, x_send, x_recv)
    v_gather = (vw, v_send, v_recv)
    w_gather = (wg, w_send, w_recv)

    def rows(py, first, count):
        return pl.ds(pl.multiple_of(py * 64 + first, 16), count)

    def h_copy(k, n):
        sems = (h_send.at[k, n], h_recv.at[k, n])
        if n == 0:
            return remote(part.at[k, rows(y2, 0, 32)], r1.at[k, 0], *sems, at_y(y1))
        if n == 1:
            return remote(part.at[k, rows(y2, 32, 32)], r1.at[k, 1], *sems, at_y(y3))
        if n == 2:
            return remote(part.at[k, rows(y1, 32, 32)], r2.at[k, 0, pl.ds(32, 32)], *sems, at_y(y1))
        if n == 3:
            return remote(part.at[k, rows(y3, 0, 32)], r2.at[k, 1, pl.ds(0, 32)], *sems, at_y(y3))
        if n == 4:
            return remote(part.at[k, rows(y1, 0, 32)], r2.at[k, 0, pl.ds(0, 32)], *sems, at_y(y1))
        if n == 5:
            return remote(part.at[k, rows(y3, 32, 32)], r2.at[k, 1, pl.ds(32, 32)], *sems, at_y(y3))
        if n < 9:
            d = n - 5
            piece = part.at[k, rows(y, lax.rem(zh + d, 4) * 16, 16)]
            return remote(piece, r3.at[k, d - 1], *sems, at_zh(d))
        if n < 12:
            d = n - 8
            piece = hid.at[k, rows(y, zh * 16, 16)]
            return remote(piece, piece, *sems, at_zh(d))
        if n == 12:
            piece, to = hid.at[k, rows(y, 0, 32)], at_y(y1)
        elif n == 13:
            piece, to = hid.at[k, rows(y, 32, 32)], at_y(y3)
        elif n == 14:
            piece, to = hid.at[k, rows(y, 32, 32)], at_y(y1)
        elif n == 15:
            piece, to = hid.at[k, rows(y, 0, 32)], at_y(y3)
        elif n == 16:
            piece, to = hid.at[k, rows(y3, 0, 32)], at_y(y1)
        else:
            piece, to = hid.at[k, rows(y1, 32, 32)], at_y(y3)
        return remote(piece, piece, *sems, to)

    def h_wait(k, n):
        if n == 0:
            dst = r1.at[k, 0]
        elif n == 1:
            dst = r1.at[k, 1]
        elif n in (2, 4):
            dst = r2.at[k, 0, pl.ds(32 if n == 2 else 0, 32)]
        elif n in (3, 5):
            dst = r2.at[k, 1, pl.ds(0 if n == 3 else 32, 32)]
        elif n < 9:
            dst = r3.at[k, n - 6]
        elif n < 12:
            dst = hid.at[k, rows(y, lax.rem(zh + 4 - (n - 8), 4) * 16, 16)]
        elif n == 12:
            dst = hid.at[k, rows(y3, 0, 32)]
        elif n == 13:
            dst = hid.at[k, rows(y1, 32, 32)]
        elif n == 14:
            dst = hid.at[k, rows(y3, 32, 32)]
        elif n == 15:
            dst = hid.at[k, rows(y1, 0, 32)]
        elif n == 16:
            dst = hid.at[k, rows(y2, 0, 32)]
        else:
            dst = hid.at[k, rows(y2, 32, 32)]
        remote(dst, dst, h_send.at[k, n], h_recv.at[k, n], at_y(y1)).wait_recv()

    def stage_partial(k):
        gather_wait_core(*x_gather, k)
        first = place(k)
        for p in range(2):
            rows_in = xg[pl.ds(first, 2), p].reshape(256, 640)
            part[k, :, pl.ds(p * 640, 640)] = dot_nt(rows_in, vh[p]).astype(BF16)
        for n in (0, 1, 2, 3):
            h_copy(k, n).start()

    def stage_near(k):
        h_wait(k, 0)
        span = rows(y1, 0, 32)
        part[k, span, :] = (part[k, span, :].astype(F32) + r1[k, 0].astype(F32)).astype(BF16)
        h_copy(k, 4).start()
        h_wait(k, 1)
        span = rows(y3, 32, 32)
        part[k, span, :] = (part[k, span, :].astype(F32) + r1[k, 1].astype(F32)).astype(BF16)
        h_copy(k, 5).start()

    def stage_own(k):
        for n in (2, 3, 4, 5):
            h_wait(k, n)
        span = rows(y, 0, 64)
        total = part[k, span, :].astype(F32) + r2[k, 0].astype(F32) + r2[k, 1].astype(F32)
        part[k, span, :] = total.astype(BF16)
        for n in (7, 6, 8):
            h_copy(k, n).start()

    def stage_sum(k):
        for n in (6, 7, 8):
            h_wait(k, n)
        span = rows(y, zh * 16, 16)
        total = part[k, span, :].astype(F32)
        for d in range(3):
            total = total + r3[k, d].astype(F32)
        hid[k, span, :] = total.astype(BF16)
        for n in (10, 9, 11):
            h_copy(k, n).start()

    def stage_spread(k):
        for n in (9, 10, 11):
            h_wait(k, n)
        for n in (12, 13, 14, 15):
            h_copy(k, n).start()

    def stage_forward(k):
        h_wait(k, 12)
        h_copy(k, 16).start()
        h_wait(k, 13)
        h_copy(k, 17).start()

    def stage_arrive(k):
        for n in (14, 15, 16, 17):
            h_wait(k, n)

    def width_part(k):
        gather_wait_core(*v_gather, k)
        first = place(k)
        span = pl.ds(pl.multiple_of(first // 2 * 640, 640), 640)
        for p in range(2):
            block = feat[p, :, span]
            add = dot_nt(block[:, :320], vw[first, p]) + dot_nt(block[:, 320:], vw[first + 1, p])
            wacc[p] = wacc[p] + add

    def prepare(n):
        p = n // 3
        j = lax.rem(n, 3)

        def body(r, _):
            span = pl.ds(pl.multiple_of(r * 64, 64), 64)
            scale = 1.0 / (eigen[p, span, :] + DAMPING)
            even = (query[p, 2 * j, span, :].astype(F32) * scale).astype(BF16)
            odd = (query[p, 2 * j + 1, span, :].astype(F32) * scale).astype(BF16)
            mult[p, j, span, :] = jnp.concatenate([even, odd], axis=1)
            return 0

        lax.fori_loop(0, 10, body, 0)

    lane = lax.broadcasted_iota(jnp.int32, (256, 128), 1)

    def score(k):
        first = place(k)
        twice = []
        for p in range(2):
            w = wg[pl.ds(first, 2), p].reshape(256, 320).astype(F32)
            twice.append(jnp.concatenate([w, w], axis=1))

        def body(j, table):
            total = jnp.zeros((256, 640), F32)
            for p in range(2):
                product = jnp.dot(
                    hid[k, :, pl.ds(p * 640, 640)], mult[p, j], preferred_element_type=F32
                )
                total = total + product * twice[p]
            tiles = [total[:, n * 128:(n + 1) * 128] for n in range(5)]
            even = tiles[0] + tiles[1] + jnp.where(lane < 64, tiles[2], 0.0)
            odd = tiles[3] + tiles[4] + jnp.where(lane < 64, 0.0, tiles[2])
            even = jnp.sum(even, axis=1, keepdims=True)
            odd = jnp.sum(odd, axis=1, keepdims=True)
            return table + jnp.where(lane == 2 * j, even, 0.0) + jnp.where(lane == 2 * j + 1, odd, 0.0)

        table = lax.fori_loop(0, 3, body, jnp.zeros((256, 128), F32))
        flat = jnp.transpose(table)[:8]
        px, pzl = first // 4, lax.rem(first // 2, 2)
        acc[0, pzl, px] = flat[:, :128]
        acc[1, pzl, px] = flat[:, 128:]

    wacc[...] = jnp.zeros_like(wacc)
    for n in (0, 1):
        loads[n].wait()
    gather_send(*x_gather, 0)
    for n in (4, 5):
        loads[n].wait()
    gather_send(*v_gather, 0)
    for n in (2, 3, 6, 7, 8, 9, 10, 11):
        loads[n].wait()

    def at(i, offset, stage):
        @pl.when((i >= offset) & (i < offset + GROUPS))
        def _():
            stage(i - offset)

    def x_step(k):
        @pl.when(k > 0)
        def _():
            gather_step(*x_gather, k)

    def v_step(k):
        @pl.when(k > 0)
        def _():
            gather_step(*v_gather, k)

    def iteration(i, _):
        at(i, 0, x_step)
        at(i, 0, stage_partial)
        at(i, 1, stage_near)
        at(i, 2, stage_own)

        @pl.when((i >= 1) & (i < 7))
        def _():
            prepare(i - 1)

        at(i, 2, v_step)
        at(i, 3, stage_sum)
        at(i, 3, width_part)
        at(i, 4, stage_spread)
        at(i, 5, stage_forward)
        at(i, 6, stage_arrive)

        @pl.when(i == 10)
        def _():
            wg[s] = wacc[...].astype(BF16)
            gather_send(*w_gather, 0)

        @pl.when(i == 11)
        def _():
            gather_step(*w_gather, 1)

        @pl.when(i == 12)
        def _():
            def body(k, _):
                gather_step(*w_gather, k)
                return 0

            lax.fori_loop(2, GROUPS, body, 0)

            def twin(k, _):
                gather_wait_core(*w_gather, k)
                return 0

            lax.fori_loop(0, GROUPS, twin, 0)

        @pl.when(i >= 12)
        def _():
            def body(k, _):
                score(k)
                return 0

            low = jnp.where(i == 12, 0, i - 6)
            high = jnp.where(i > 13, 0, i - 5)
            lax.fori_loop(low, high, body, 0)

        return 0

    lax.fori_loop(0, 14, iteration, 0)

    copy = remote(acc.at[1 - c], red_c, red_send.at[0], red_recv.at[0], to_core)
    copy.start()
    copy.wait()
    acc[c] = acc[c] + red_c[...]
    copy = remote(acc.at[c, 1 - zl], red_zl, red_send.at[1], red_recv.at[1], to_zl)
    copy.start()
    copy.wait()
    acc[c, zl] = acc[c, zl] + red_zl[...]
    copies = [
        remote(acc.at[c, zl, px], red_x.at[n], red_send.at[2 + n], red_recv.at[2 + n], at_x(px))
        for n, px in enumerate((x1, x2, x3))
    ]
    for copy in copies:
        copy.start()
    for copy in copies:
        copy.wait()
    sum_x[...] = acc[c, zl, x] + red_x[0] + red_x[1] + red_x[2]
    copies = [
        remote(sum_x, red_y.at[n], red_send.at[5 + n], red_recv.at[5 + n], at_y(py))
        for n, py in enumerate((y1, y2, y3))
    ]
    for copy in copies:
        copy.start()
    for copy in copies:
        copy.wait()
    sum_y[...] = sum_x[...] + red_y[0] + red_y[1] + red_y[2]
    copies = [
        remote(sum_y, red_zh.at[n], red_send.at[8 + n], red_recv.at[8 + n], at_zh(n + 1))
        for n in range(3)
    ]
    for copy in copies:
        copy.start()
    for copy in copies:
        copy.wait()
    out[...] = (sum_y[...] + red_zh[0] + red_zh[1] + red_zh[2])[:6]

    for gather in (x_gather, v_gather, w_gather):
        gather_drain(*gather)

    def drain(k, _):
        for n in range(18):
            h_copy(k, n).wait_send()
        return 0

    lax.fori_loop(0, GROUPS, drain, 0)


def shards(*blocks):
    vmem = pltpu.VMEM
    return pl.pallas_call(
        kernel,
        out_shape=jax.ShapeDtypeStruct((6, 128), F32),
        in_specs=[pl.BlockSpec(memory_space=pl.ANY)] * 12,
        out_specs=pl.BlockSpec(memory_space=pltpu.VMEM),
        scratch_shapes=[
            vmem((16, 2, 128, 640), BF16),
            vmem((2, 640, 640), BF16),
            vmem((GROUPS, 256, 1280), BF16),
            vmem((GROUPS, 2, 32, 1280), BF16),
            vmem((GROUPS, 2, 64, 1280), BF16),
            vmem((GROUPS, 3, 16, 1280), BF16),
            vmem((GROUPS, 256, 1280), BF16),
            vmem((16, 2, 320, 320), BF16),
            vmem((2, 128, 5120), BF16),
            vmem((2, 128, 320), F32),
            vmem((16, 2, 128, 320), BF16),
            vmem((2, 6, 640, 320), BF16),
            vmem((2, 640, 320), F32),
            vmem((2, 3, 640, 640), BF16),
            vmem((2, 2, 4, 8, 128), F32),
            vmem((2, 4, 8, 128), F32),
            vmem((4, 8, 128), F32),
            vmem((3, 8, 128), F32),
            vmem((3, 8, 128), F32),
            vmem((3, 8, 128), F32),
            vmem((8, 128), F32),
            vmem((8, 128), F32),
            pltpu.SemaphoreType.DMA((12,)),
            pltpu.SemaphoreType.DMA((4, GROUPS)),
            pltpu.SemaphoreType.DMA((16,)),
            pltpu.SemaphoreType.DMA((4, GROUPS)),
            pltpu.SemaphoreType.DMA((16,)),
            pltpu.SemaphoreType.DMA((4, GROUPS)),
            pltpu.SemaphoreType.DMA((16,)),
            pltpu.SemaphoreType.DMA((GROUPS, 18)),
            pltpu.SemaphoreType.DMA((GROUPS, 18)),
            pltpu.SemaphoreType.DMA((11,)),
            pltpu.SemaphoreType.DMA((11,)),
        ],
        compiler_params=pltpu.CompilerParams(
            collective_id=0, has_side_effects=True, vmem_limit_bytes=60 * 1024 * 1024
        ),
        cost_estimate=pl.CostEstimate(flops=14_000_000_000, bytes_accessed=12_000_000, transcendentals=0),
    )(*blocks)


def solution(mesh):
    return jax.shard_map(
        shards,
        mesh=mesh,
        in_specs=(
            P("seq", None),
            P("seq", "basis"),
            P("seq", "basis"),
            P("seq", None),
            P("basis", "seq"),
            P("basis", "seq"),
            P("seq", "basis"),
            P("seq", "basis"),
            P(None, "seq", "basis"),
            P(None, "seq", "basis"),
            P("seq", "basis"),
            P("seq", "basis"),
        ),
        out_specs=P(None, "seq"),
        check_vma=False,
    )
```

```python
import functools

import jax
import jax.numpy as jnp
from jax import lax
from jax.experimental import pallas as pl
from jax.experimental.pallas import tpu as pltpu
from jax.sharding import PartitionSpec as P

DAMPING = 0.1
MESH = pl.DeviceIdType.MESH
F32 = jnp.float32
BF16 = jnp.bfloat16

GROUPS = 8
ORDER = "gfedcbaws"
O_X, O_PART, O_NEAR, O_OWN, O_SUM, O_SPREAD, O_FORWARD, O_ARRIVE, O_SCORE = 0, 0, 1, 2, 3, 4, 5, 6, 9
RATE = 2
V_MARKS = ((2, 2), (3, 4), (5, 6), (6, 8))
VC_MARKS = ((3, 2), (4, 4), (6, 6), (7, 8))
W_START = 7
W_MARKS = ((8, 2), (9, 8))
WC_MARKS = ((9, 8),)


def dot_nt(a, b):
    return lax.dot_general(a, b, (((1,), (1,)), ((), ())), preferred_element_type=F32)


def kernel(
    up_input, up_grad, down_input, down_grad, width_up, width_down, hidden_up, hidden_down,
    query_up, query_down, eigen_up, eigen_down,
    out,
    xg, vh, part, r1, r2, r3, hid, vw, feat, wacc, wg, query, eigen, mult,
    acc, red_c, red_zl, red_x, red_y, red_zh, sum_x, sum_y,
    local_sem, x_send, x_recv, v_send, v_recv, w_send, w_recv,
    h_send, h_recv, red_send, red_recv,
):
    s = lax.axis_index("seq")
    b = lax.axis_index("basis")
    x, zl, c = s // 4, lax.rem(s // 2, 2), lax.rem(s, 2)
    zh, y = b // 4, lax.rem(b, 4)
    x1, x2, x3 = lax.rem(x + 1, 4), lax.rem(x + 2, 4), lax.rem(x + 3, 4)
    y1, y2, y3 = lax.rem(y + 1, 4), lax.rem(y + 2, 4), lax.rem(y + 3, 4)

    def slot(px, pzl, pc):
        return px * 4 + pzl * 2 + pc

    def at_y(py):
        return (s, zh * 4 + py)

    def at_zh(d):
        return (s, lax.rem(zh + d, 4) * 4 + y)

    def at_x(px):
        return (slot(px, zl, c), b)

    to_core = (slot(x, zl, 1 - c), b)
    to_zl = (slot(x, 1 - zl, c), b)

    def remote(src, dst, send, recv, to):
        return pltpu.make_async_remote_copy(
            src_ref=src, dst_ref=dst, send_sem=send, recv_sem=recv, device_id=to, device_id_type=MESH
        )

    moves = [
        (up_grad, xg.at[s, 0]),
        (down_input, xg.at[s, 1]),
        (hidden_up, vh.at[0]),
        (hidden_down, vh.at[1]),
        (width_up, vw.at[s, 0]),
        (width_down, vw.at[s, 1]),
        (query_up, query.at[0]),
        (query_down, query.at[1]),
        (eigen_up, eigen.at[0]),
        (eigen_down, eigen.at[1]),
        (up_input, feat.at[0]),
        (down_grad, feat.at[1]),
    ]
    loads = [pltpu.make_async_copy(a, d, local_sem.at[n]) for n, (a, d) in enumerate(moves)]
    for load in loads:
        load.start()

    barrier = pltpu.get_barrier_semaphore()
    partners = [to_core, to_zl, at_x(x1), at_x(x2), at_x(x3), at_y(y1), at_y(y2), at_y(y3)]
    partners += [at_zh(d) for d in (1, 2, 3)]
    for partner in partners:
        pl.semaphore_signal(barrier, inc=1, device_id=partner, device_id_type=MESH)
    pl.semaphore_wait(barrier, len(partners))

    def place(k):
        px = jnp.where(k < 2, x, jnp.where(k >= 6, x2, jnp.where(lax.rem(k, 2) == 0, x3, x1)))
        own = (k == 0) | (k == 2) | (k == 3) | (k == 6)
        return px * 4 + jnp.where(own, zl, 1 - zl) * 2

    def gather_copy(buf, send, recv, k, way, to):
        block = buf.at[place(k) + c]
        return remote(block, block, send.at[way, k], recv.at[place(k) + c], to)

    def gather_send(buf, send, recv, k):
        gather_copy(buf, send, recv, k, 0, to_core).start()

        @pl.when(k == 0)
        def _():
            gather_copy(buf, send, recv, k, 1, to_zl).start()

        @pl.when(k <= 2)
        def _():
            gather_copy(buf, send, recv, k, 2, at_x(x1)).start()

        @pl.when((k <= 1) | (k == 5))
        def _():
            gather_copy(buf, send, recv, k, 3, at_x(x3)).start()

    def gather_wait(buf, send, recv, k):
        gather_copy(buf, send, recv, k, 0, to_core).wait_recv()

    def gather_wait_core(buf, send, recv, k):
        block = buf.at[place(k) + 1 - c]
        remote(block, block, send.at[0, k], recv.at[place(k) + 1 - c], to_core).wait_recv()

    def gather_step(buf, send, recv, k):
        @pl.when(k > 0)
        def _():
            gather_wait(buf, send, recv, k)

        gather_send(buf, send, recv, k)

    def gather_drain(buf, send, recv):
        def body(k, _):
            gather_copy(buf, send, recv, k, 0, to_core).wait_send()

            @pl.when(k == 0)
            def _():
                gather_copy(buf, send, recv, k, 1, to_zl).wait_send()

            @pl.when(k <= 2)
            def _():
                gather_copy(buf, send, recv, k, 2, at_x(x1)).wait_send()

            @pl.when((k <= 1) | (k == 5))
            def _():
                gather_copy(buf, send, recv, k, 3, at_x(x3)).wait_send()

            return 0

        lax.fori_loop(0, GROUPS, body, 0)

    x_gather = (xg, x_send, x_recv)
    v_gather = (vw, v_send, v_recv)
    w_gather = (wg, w_send, w_recv)

    def rows(py, first, count):
        return pl.ds(pl.multiple_of(py * 64 + first, 16), count)

    def h_copy(k, n):
        sems = (h_send.at[k, n], h_recv.at[k, n])
        if n == 0:
            return remote(part.at[k, rows(y2, 0, 32)], r1.at[k, 0], *sems, at_y(y1))
        if n == 1:
            return remote(part.at[k, rows(y2, 32, 32)], r1.at[k, 1], *sems, at_y(y3))
        if n == 2:
            return remote(part.at[k, rows(y1, 32, 32)], r2.at[k, 0, pl.ds(32, 32)], *sems, at_y(y1))
        if n == 3:
            return remote(part.at[k, rows(y3, 0, 32)], r2.at[k, 1, pl.ds(0, 32)], *sems, at_y(y3))
        if n == 4:
            return remote(part.at[k, rows(y1, 0, 32)], r2.at[k, 0, pl.ds(0, 32)], *sems, at_y(y1))
        if n == 5:
            return remote(part.at[k, rows(y3, 32, 32)], r2.at[k, 1, pl.ds(32, 32)], *sems, at_y(y3))
        if n < 9:
            d = n - 5
            piece = part.at[k, rows(y, lax.rem(zh + d, 4) * 16, 16)]
            return remote(piece, r3.at[k, d - 1], *sems, at_zh(d))
        if n < 12:
            d = n - 8
            piece = hid.at[k, rows(y, zh * 16, 16)]
            return remote(piece, piece, *sems, at_zh(d))
        if n == 12:
            piece, to = hid.at[k, rows(y, 0, 32)], at_y(y1)
        elif n == 13:
            piece, to = hid.at[k, rows(y, 32, 32)], at_y(y3)
        elif n == 14:
            piece, to = hid.at[k, rows(y, 32, 32)], at_y(y1)
        elif n == 15:
            piece, to = hid.at[k, rows(y, 0, 32)], at_y(y3)
        elif n == 16:
            piece, to = hid.at[k, rows(y3, 0, 32)], at_y(y1)
        else:
            piece, to = hid.at[k, rows(y1, 32, 32)], at_y(y3)
        return remote(piece, piece, *sems, to)

    def h_wait(k, n):
        if n == 0:
            dst = r1.at[k, 0]
        elif n == 1:
            dst = r1.at[k, 1]
        elif n in (2, 4):
            dst = r2.at[k, 0, pl.ds(32 if n == 2 else 0, 32)]
        elif n in (3, 5):
            dst = r2.at[k, 1, pl.ds(0 if n == 3 else 32, 32)]
        elif n < 9:
            dst = r3.at[k, n - 6]
        elif n < 12:
            dst = hid.at[k, rows(y, lax.rem(zh + 4 - (n - 8), 4) * 16, 16)]
        elif n == 12:
            dst = hid.at[k, rows(y3, 0, 32)]
        elif n == 13:
            dst = hid.at[k, rows(y1, 32, 32)]
        elif n == 14:
            dst = hid.at[k, rows(y3, 32, 32)]
        elif n == 15:
            dst = hid.at[k, rows(y1, 0, 32)]
        elif n == 16:
            dst = hid.at[k, rows(y2, 0, 32)]
        else:
            dst = hid.at[k, rows(y2, 32, 32)]
        remote(dst, dst, h_send.at[k, n], h_recv.at[k, n], at_y(y1)).wait_recv()

    def stage_partial(k):
        gather_wait_core(*x_gather, k)
        first = place(k)
        for p in range(2):
            rows_in = xg[pl.ds(first, 2), p].reshape(256, 640)
            part[k, :, pl.ds(p * 640, 640)] = dot_nt(rows_in, vh[p]).astype(BF16)
        for n in (0, 1, 2, 3):
            h_copy(k, n).start()

    def stage_near(k):
        h_wait(k, 0)
        span = rows(y1, 0, 32)
        part[k, span, :] = (part[k, span, :].astype(F32) + r1[k, 0].astype(F32)).astype(BF16)
        h_copy(k, 4).start()
        h_wait(k, 1)
        span = rows(y3, 32, 32)
        part[k, span, :] = (part[k, span, :].astype(F32) + r1[k, 1].astype(F32)).astype(BF16)
        h_copy(k, 5).start()

    def stage_own(k):
        for n in (2, 3, 4, 5):
            h_wait(k, n)
        span = rows(y, 0, 64)
        total = part[k, span, :].astype(F32) + r2[k, 0].astype(F32) + r2[k, 1].astype(F32)
        part[k, span, :] = total.astype(BF16)
        for n in (7, 6, 8):
            h_copy(k, n).start()

    def stage_sum(k):
        for n in (6, 7, 8):
            h_wait(k, n)
        span = rows(y, zh * 16, 16)
        total = part[k, span, :].astype(F32)
        for d in range(3):
            total = total + r3[k, d].astype(F32)
        hid[k, span, :] = total.astype(BF16)
        for n in (10, 9, 11):
            h_copy(k, n).start()

    def stage_spread(k):
        for n in (9, 10, 11):
            h_wait(k, n)
        for n in (12, 13, 14, 15):
            h_copy(k, n).start()

    def stage_forward(k):
        h_wait(k, 12)
        h_copy(k, 16).start()
        h_wait(k, 13)
        h_copy(k, 17).start()

    def stage_arrive(k):
        for n in (14, 15, 16, 17):
            h_wait(k, n)

    def width_part(k):
        gather_wait_core(*v_gather, k)
        first = place(k)
        span = pl.ds(pl.multiple_of(first // 2 * 640, 640), 640)
        for p in range(2):
            block = feat[p, :, span]
            add = dot_nt(block[:, :320], vw[first, p]) + dot_nt(block[:, 320:], vw[first + 1, p])
            wacc[p] = wacc[p] + add

    def prepare(p):
        def body(r, _):
            span = pl.ds(pl.multiple_of(r * 32, 32), 32)
            scale = 1.0 / (eigen[p, span, :] + DAMPING)
            for q in range(6):
                mult[p, q, span, :] = (query[p, q, span, :].astype(F32) * scale).astype(BF16)
            return 0

        lax.fori_loop(0, 10, body, 0)

    lane = lax.broadcasted_iota(jnp.int32, (256, 128), 1)

    def score(k):
        first = place(k)
        twice = []
        for p in range(2):
            w = wg[pl.ds(first, 2), p].reshape(256, 320).astype(F32)
            twice.append(jnp.concatenate([w, w], axis=1))

        def body(j, table):
            total = jnp.zeros((256, 640), F32)
            for p in range(2):
                product = dot_nt(
                    hid[k, :, pl.ds(p * 640, 640)], mult[p, pl.ds(2 * j, 2)].reshape(640, 640)
                )
                total = total + product * twice[p]
            tiles = [total[:, n * 128:(n + 1) * 128] for n in range(5)]
            even = tiles[0] + tiles[1] + jnp.where(lane < 64, tiles[2], 0.0)
            odd = tiles[3] + tiles[4] + jnp.where(lane < 64, 0.0, tiles[2])
            even = jnp.sum(even, axis=1, keepdims=True)
            odd = jnp.sum(odd, axis=1, keepdims=True)
            return table + jnp.where(lane == 2 * j, even, 0.0) + jnp.where(lane == 2 * j + 1, odd, 0.0)

        table = lax.fori_loop(0, 3, body, jnp.zeros((256, 128), F32))
        flat = jnp.transpose(table)[:8]
        px, pzl = first // 4, lax.rem(first // 2, 2)
        acc[0, pzl, px] = flat[:, :128]
        acc[1, pzl, px] = flat[:, 128:]

    wacc[...] = jnp.zeros_like(wacc)
    for n in (0, 1):
        loads[n].wait()
    gather_send(*x_gather, 0)
    for n in (4, 5):
        loads[n].wait()
    gather_send(*v_gather, 0)
    for n in (2, 3):
        loads[n].wait()

    def at(i, offset, stage):
        @pl.when((i >= offset) & (i < offset + GROUPS))
        def _():
            stage(i - offset)

    def loop(low, high, stage):
        def body(k, _):
            stage(k)
            return 0

        lax.fori_loop(low, high, body, 0)

    def x_step(k):
        @pl.when(k > 0)
        def _():
            gather_step(*x_gather, k)

    def v_step(k):
        gather_step(*v_gather, k)

    def w_step(k):
        gather_step(*w_gather, k)

    def w_twin(k):
        gather_wait_core(*w_gather, k)

    def bounds(i, marks):
        low, high = 0, 0
        for mark, value in marks:
            low = jnp.where(i > mark, value, low)
            high = jnp.where(i >= mark, value, high)
        return low, high

    def run_width(i):
        low, high = bounds(i, V_MARKS)
        loop(jnp.maximum(low, 1), high, v_step)
        low, high = bounds(i, VC_MARKS)
        loop(low, high, width_part)

        @pl.when(i == W_START)
        def _():
            wg[s] = wacc[...].astype(BF16)
            gather_send(*w_gather, 0)

        low, high = bounds(i, W_MARKS)
        loop(jnp.maximum(low, 1), high, w_step)
        low, high = bounds(i, WC_MARKS)
        loop(low, high, w_twin)

    def run_score(i):
        def done(n):
            return jnp.clip(jnp.minimum(n - O_ARRIVE + 1, RATE * (n - O_SCORE + 1)), 0, GROUPS)

        loop(done(i - 1), done(i), score)

    def iteration(i, _):
        for stage in ORDER:
            if stage == "a":
                at(i, O_X, x_step)
                at(i, O_PART, stage_partial)
            if stage == "b":
                at(i, O_NEAR, stage_near)
            if stage == "c":
                at(i, O_OWN, stage_own)
            if stage == "d":
                at(i, O_SUM, stage_sum)
            if stage == "e":
                at(i, O_SPREAD, stage_spread)
            if stage == "f":
                at(i, O_FORWARD, stage_forward)
            if stage == "g":
                at(i, O_ARRIVE, stage_arrive)
            if stage == "w":
                run_width(i)
            if stage == "s":
                run_score(i)

        @pl.when(i == 0)
        def _():
            for n in (6, 7, 8, 9, 10, 11):
                loads[n].wait()

        @pl.when((i == 2) | (i == 3))
        def _():
            prepare(i - 2)

        return 0

    lax.fori_loop(0, O_ARRIVE + GROUPS, iteration, 0)

    copy = remote(acc.at[1 - c], red_c, red_send.at[0], red_recv.at[0], to_core)
    copy.start()
    copy.wait()
    acc[c] = acc[c] + red_c[...]
    copy = remote(acc.at[c, 1 - zl], red_zl, red_send.at[1], red_recv.at[1], to_zl)
    copy.start()
    copy.wait()
    acc[c, zl] = acc[c, zl] + red_zl[...]
    copies = [
        remote(acc.at[c, zl, px], red_x.at[n], red_send.at[2 + n], red_recv.at[2 + n], at_x(px))
        for n, px in enumerate((x1, x2, x3))
    ]
    for copy in copies:
        copy.start()
    for copy in copies:
        copy.wait()
    sum_x[...] = acc[c, zl, x] + red_x[0] + red_x[1] + red_x[2]
    copies = [
        remote(sum_x, red_y.at[n], red_send.at[5 + n], red_recv.at[5 + n], at_y(py))
        for n, py in enumerate((y1, y2, y3))
    ]
    for copy in copies:
        copy.start()
    for copy in copies:
        copy.wait()
    sum_y[...] = sum_x[...] + red_y[0] + red_y[1] + red_y[2]
    copies = [
        remote(sum_y, red_zh.at[n], red_send.at[8 + n], red_recv.at[8 + n], at_zh(n + 1))
        for n in range(3)
    ]
    for copy in copies:
        copy.start()
    for copy in copies:
        copy.wait()
    out[...] = (sum_y[...] + red_zh[0] + red_zh[1] + red_zh[2])[:6]

    for gather in (x_gather, v_gather, w_gather):
        gather_drain(*gather)

    def drain(k, _):
        for n in range(18):
            h_copy(k, n).wait_send()
        return 0

    lax.fori_loop(0, GROUPS, drain, 0)


def shards(*blocks):
    vmem = pltpu.VMEM
    blocks = blocks[:8] + tuple(jnp.swapaxes(block, -1, -2) for block in blocks[8:])
    return pl.pallas_call(
        kernel,
        out_shape=jax.ShapeDtypeStruct((6, 128), F32),
        in_specs=[pl.BlockSpec(memory_space=pl.ANY)] * 12,
        out_specs=pl.BlockSpec(memory_space=pltpu.VMEM),
        scratch_shapes=[
            vmem((16, 2, 128, 640), BF16),
            vmem((2, 640, 640), BF16),
            vmem((GROUPS, 256, 1280), BF16),
            vmem((GROUPS, 2, 32, 1280), BF16),
            vmem((GROUPS, 2, 64, 1280), BF16),
            vmem((GROUPS, 3, 16, 1280), BF16),
            vmem((GROUPS, 256, 1280), BF16),
            vmem((16, 2, 320, 320), BF16),
            vmem((2, 128, 5120), BF16),
            vmem((2, 128, 320), F32),
            vmem((16, 2, 128, 320), BF16),
            vmem((2, 6, 320, 640), BF16),
            vmem((2, 320, 640), F32),
            vmem((2, 6, 320, 640), BF16),
            vmem((2, 2, 4, 8, 128), F32),
            vmem((2, 4, 8, 128), F32),
            vmem((4, 8, 128), F32),
            vmem((3, 8, 128), F32),
            vmem((3, 8, 128), F32),
            vmem((3, 8, 128), F32),
            vmem((8, 128), F32),
            vmem((8, 128), F32),
            pltpu.SemaphoreType.DMA((12,)),
            pltpu.SemaphoreType.DMA((4, GROUPS)),
            pltpu.SemaphoreType.DMA((16,)),
            pltpu.SemaphoreType.DMA((4, GROUPS)),
            pltpu.SemaphoreType.DMA((16,)),
            pltpu.SemaphoreType.DMA((4, GROUPS)),
            pltpu.SemaphoreType.DMA((16,)),
            pltpu.SemaphoreType.DMA((GROUPS, 18)),
            pltpu.SemaphoreType.DMA((GROUPS, 18)),
            pltpu.SemaphoreType.DMA((11,)),
            pltpu.SemaphoreType.DMA((11,)),
        ],
        compiler_params=pltpu.CompilerParams(
            collective_id=0, has_side_effects=True, vmem_limit_bytes=60 * 1024 * 1024
        ),
        cost_estimate=pl.CostEstimate(flops=14_000_000_000, bytes_accessed=12_000_000, transcendentals=0),
    )(*blocks)


def solution(mesh):
    return jax.shard_map(
        shards,
        mesh=mesh,
        in_specs=(
            P("seq", None),
            P("seq", "basis"),
            P("seq", "basis"),
            P("seq", None),
            P("basis", "seq"),
            P("basis", "seq"),
            P("seq", "basis"),
            P("seq", "basis"),
            P(None, "seq", "basis"),
            P(None, "seq", "basis"),
            P("seq", "basis"),
            P("seq", "basis"),
        ),
        out_specs=P(None, "seq"),
        check_vma=False,
    )
```

```python
import functools

import jax
import jax.numpy as jnp
from jax import lax
from jax.experimental import pallas as pl
from jax.experimental.pallas import tpu as pltpu
from jax.sharding import PartitionSpec as P

DAMPING = 0.1
MESH = pl.DeviceIdType.MESH
F32 = jnp.float32
BF16 = jnp.bfloat16

N_SEQ, N_BASIS = 16, 16
GROUPS = 8
ORDER = "gfedcbawsws"
O_X, O_PART, O_NEAR, O_OWN, O_SUM, O_SPREAD, O_FORWARD, O_ARRIVE = 0, 0, 1, 2, 3, 4, 5, 6
VB_START = 3
VA_MARKS = ((0, 1), (5, 2), (7, 4), (11, 6), (13, 8))
VB_MARKS = ((0, 1), (9, 2), (11, 4), (15, 6), (17, 8))
VAC_MARKS = ((0, 0), (7, 2), (9, 4), (13, 6), (15, 8))
VBC_MARKS = ((0, 0), (13, 2), (15, 4), (17, 6), (19, 8))
WU_START = 15
WU_MARKS = ((0, 1), (17, 2), (18, 6), (19, 8))
WUC_MARKS = ((0, 0), (19, 8))
WD_START = 19
WD_MARKS = ((0, 1), (20, 2), (21, 6), (22, 8))
WDC_MARKS = ((0, 0), (22, 8))
SU_START = 19
SD_START = 22
RATE = 2


def dot_nt(a, b):
    return lax.dot_general(a, b, (((1,), (1,)), ((), ())), preferred_element_type=F32)


def kernel(
    up_input, up_grad, down_input, down_grad, width_up, width_down, hidden_up, hidden_down,
    query_up, query_down, eigen_up, eigen_down,
    out,
    xg, vh, part, r1, r2, r3, hid, wide, va, vb, feat, wacc, wu, wd, query, eigen, mult,
    half, acc, seq_in, seq_sum, basis_in,
    local_sem, x_send, x_recv, g_send, g_recv,
    h_send, h_recv, seq_send, seq_recv, basis_send, basis_recv,
):
    s = lax.axis_index("seq")
    b = lax.axis_index("basis")
    x, zl, c = s // 4, lax.rem(s // 2, 2), lax.rem(s, 2)
    zh, y = b // 4, lax.rem(b, 4)
    x1, x2, x3 = lax.rem(x + 1, 4), lax.rem(x + 2, 4), lax.rem(x + 3, 4)
    y1, y2, y3 = lax.rem(y + 1, 4), lax.rem(y + 2, 4), lax.rem(y + 3, 4)

    def slot(px, pzl, pc):
        return px * 4 + pzl * 2 + pc

    def at_y(py):
        return (s, zh * 4 + py)

    def at_zh(d):
        return (s, lax.rem(zh + d, 4) * 4 + y)

    def at_x(px):
        return (slot(px, zl, c), b)

    to_core = (slot(x, zl, 1 - c), b)
    to_zl = (slot(x, 1 - zl, c), b)

    def remote(src, dst, send, recv, to):
        return pltpu.make_async_remote_copy(
            src_ref=src, dst_ref=dst, send_sem=send, recv_sem=recv, device_id=to, device_id_type=MESH
        )

    moves = [
        (up_grad, xg.at[s, 0]),
        (down_input, xg.at[s, 1]),
        (hidden_up, vh.at[0]),
        (hidden_down, vh.at[1]),
        (width_up, wide.at[0]),
        (width_down, wide.at[1]),
        (query_up, query.at[0]),
        (query_down, query.at[1]),
        (eigen_up, eigen.at[0]),
        (eigen_down, eigen.at[1]),
        (up_input, feat.at[0]),
        (down_grad, feat.at[1]),
    ]
    loads = [pltpu.make_async_copy(a, d, local_sem.at[n]) for n, (a, d) in enumerate(moves)]
    for load in loads:
        load.start()

    barrier = pltpu.get_barrier_semaphore()
    def prepare(p):
        def body(r, _):
            span = pl.ds(pl.multiple_of(r * 32, 32), 32)
            scale = 1.0 / (eigen[p, span, :] + DAMPING)
            for q in range(6):
                mult[p, q, span, :] = (query[p, q, span, :].astype(F32) * scale).astype(BF16)
            return 0

        lax.fori_loop(0, 10, body, 0)

    others = N_SEQ + N_BASIS - 2

    def along_seq(d):
        return (lax.rem(s + d, N_SEQ), b)

    def along_basis(d):
        return (s, lax.rem(b + d, N_BASIS))

    def greet(d, _):
        pl.semaphore_signal(barrier, inc=1, device_id=along_seq(d), device_id_type=MESH)
        pl.semaphore_signal(barrier, inc=1, device_id=along_basis(d), device_id_type=MESH)
        return 0

    lax.fori_loop(1, N_SEQ, greet, 0)
    for n in (6, 7, 8, 9):
        loads[n].wait()
    prepare(0)
    prepare(1)
    for n in (4, 5):
        loads[n].wait()
    va[s] = jnp.concatenate([wide[0], wide[1, :, 256:]], axis=1)
    vb[s] = wide[1, :, :256]
    pl.semaphore_wait(barrier, others)

    def place(k):
        px = jnp.where(k < 2, x, jnp.where(k >= 6, x2, jnp.where(lax.rem(k, 2) == 0, x3, x1)))
        own = (k == 0) | (k == 2) | (k == 3) | (k == 6)
        return px * 4 + jnp.where(own, zl, 1 - zl) * 2

    def gather_copy(buf, send, recv, k, way, to):
        block = buf.at[place(k) + c]
        return remote(block, block, send.at[way, k], recv.at[place(k) + c], to)

    def gather_send(buf, send, recv, k):
        gather_copy(buf, send, recv, k, 0, to_core).start()

        @pl.when(k == 0)
        def _():
            gather_copy(buf, send, recv, k, 1, to_zl).start()

        @pl.when(k <= 2)
        def _():
            gather_copy(buf, send, recv, k, 2, at_x(x1)).start()

        @pl.when((k <= 1) | (k == 5))
        def _():
            gather_copy(buf, send, recv, k, 3, at_x(x3)).start()

    def gather_wait(buf, send, recv, k):
        gather_copy(buf, send, recv, k, 0, to_core).wait_recv()

    def gather_wait_core(buf, send, recv, k):
        block = buf.at[place(k) + 1 - c]
        remote(block, block, send.at[0, k], recv.at[place(k) + 1 - c], to_core).wait_recv()

    def gather_step(buf, send, recv, k):
        @pl.when(k > 0)
        def _():
            gather_wait(buf, send, recv, k)

        gather_send(buf, send, recv, k)

    def gather_drain(buf, send, recv):
        def body(k, _):
            gather_copy(buf, send, recv, k, 0, to_core).wait_send()

            @pl.when(k == 0)
            def _():
                gather_copy(buf, send, recv, k, 1, to_zl).wait_send()

            @pl.when(k <= 2)
            def _():
                gather_copy(buf, send, recv, k, 2, at_x(x1)).wait_send()

            @pl.when((k <= 1) | (k == 5))
            def _():
                gather_copy(buf, send, recv, k, 3, at_x(x3)).wait_send()

            return 0

        lax.fori_loop(0, GROUPS, body, 0)

    x_gather = (xg, x_send, x_recv)
    va_gather = (va, g_send.at[0], g_recv.at[0])
    vb_gather = (vb, g_send.at[1], g_recv.at[1])
    wu_gather = (wu, g_send.at[2], g_recv.at[2])
    wd_gather = (wd, g_send.at[3], g_recv.at[3])

    def rows(py, first, count):
        return pl.ds(pl.multiple_of(py * 64 + first, 16), count)

    def h_copy(k, n):
        sems = (h_send.at[k, n], h_recv.at[k, n])
        if n == 0:
            return remote(part.at[k, rows(y2, 0, 32)], r1.at[k, 0], *sems, at_y(y1))
        if n == 1:
            return remote(part.at[k, rows(y2, 32, 32)], r1.at[k, 1], *sems, at_y(y3))
        if n == 2:
            return remote(part.at[k, rows(y1, 32, 32)], r2.at[k, 0, pl.ds(32, 32)], *sems, at_y(y1))
        if n == 3:
            return remote(part.at[k, rows(y3, 0, 32)], r2.at[k, 1, pl.ds(0, 32)], *sems, at_y(y3))
        if n == 4:
            return remote(part.at[k, rows(y1, 0, 32)], r2.at[k, 0, pl.ds(0, 32)], *sems, at_y(y1))
        if n == 5:
            return remote(part.at[k, rows(y3, 32, 32)], r2.at[k, 1, pl.ds(32, 32)], *sems, at_y(y3))
        if n < 9:
            d = n - 5
            piece = part.at[k, rows(y, lax.rem(zh + d, 4) * 16, 16)]
            return remote(piece, r3.at[k, d - 1], *sems, at_zh(d))
        if n < 12:
            d = n - 8
            piece = hid.at[k, rows(y, zh * 16, 16)]
            return remote(piece, piece, *sems, at_zh(d))
        if n == 12:
            piece, to = hid.at[k, rows(y, 0, 32)], at_y(y1)
        elif n == 13:
            piece, to = hid.at[k, rows(y, 32, 32)], at_y(y3)
        elif n == 14:
            piece, to = hid.at[k, rows(y, 32, 32)], at_y(y1)
        elif n == 15:
            piece, to = hid.at[k, rows(y, 0, 32)], at_y(y3)
        elif n == 16:
            piece, to = hid.at[k, rows(y3, 0, 32)], at_y(y1)
        else:
            piece, to = hid.at[k, rows(y1, 32, 32)], at_y(y3)
        return remote(piece, piece, *sems, to)

    def h_wait(k, n):
        if n == 0:
            dst = r1.at[k, 0]
        elif n == 1:
            dst = r1.at[k, 1]
        elif n in (2, 4):
            dst = r2.at[k, 0, pl.ds(32 if n == 2 else 0, 32)]
        elif n in (3, 5):
            dst = r2.at[k, 1, pl.ds(0 if n == 3 else 32, 32)]
        elif n < 9:
            dst = r3.at[k, n - 6]
        elif n < 12:
            dst = hid.at[k, rows(y, lax.rem(zh + 4 - (n - 8), 4) * 16, 16)]
        elif n == 12:
            dst = hid.at[k, rows(y3, 0, 32)]
        elif n == 13:
            dst = hid.at[k, rows(y1, 32, 32)]
        elif n == 14:
            dst = hid.at[k, rows(y3, 32, 32)]
        elif n == 15:
            dst = hid.at[k, rows(y1, 0, 32)]
        elif n == 16:
            dst = hid.at[k, rows(y2, 0, 32)]
        else:
            dst = hid.at[k, rows(y2, 32, 32)]
        remote(dst, dst, h_send.at[k, n], h_recv.at[k, n], at_y(y1)).wait_recv()

    def stage_partial(k):
        gather_wait_core(*x_gather, k)
        first = place(k)
        for p in range(2):
            rows_in = xg[pl.ds(first, 2), p].reshape(256, 640)
            part[k, :, pl.ds(p * 640, 640)] = dot_nt(rows_in, vh[p]).astype(BF16)
        for n in (0, 1, 2, 3):
            h_copy(k, n).start()

    def stage_near(k):
        h_wait(k, 0)
        span = rows(y1, 0, 32)
        part[k, span, :] = (part[k, span, :].astype(F32) + r1[k, 0].astype(F32)).astype(BF16)
        h_copy(k, 4).start()
        h_wait(k, 1)
        span = rows(y3, 32, 32)
        part[k, span, :] = (part[k, span, :].astype(F32) + r1[k, 1].astype(F32)).astype(BF16)
        h_copy(k, 5).start()

    def stage_own(k):
        for n in (2, 3, 4, 5):
            h_wait(k, n)
        span = rows(y, 0, 64)
        total = part[k, span, :].astype(F32) + r2[k, 0].astype(F32) + r2[k, 1].astype(F32)
        part[k, span, :] = total.astype(BF16)
        for n in (7, 6, 8):
            h_copy(k, n).start()

    def stage_sum(k):
        for n in (6, 7, 8):
            h_wait(k, n)
        span = rows(y, zh * 16, 16)
        total = part[k, span, :].astype(F32)
        for d in range(3):
            total = total + r3[k, d].astype(F32)
        hid[k, span, :] = total.astype(BF16)
        for n in (10, 9, 11):
            h_copy(k, n).start()

    def stage_spread(k):
        for n in (9, 10, 11):
            h_wait(k, n)
        for n in (12, 13, 14, 15):
            h_copy(k, n).start()

    def stage_forward(k):
        h_wait(k, 12)
        h_copy(k, 16).start()
        h_wait(k, 13)
        h_copy(k, 17).start()

    def stage_arrive(k):
        for n in (14, 15, 16, 17):
            h_wait(k, n)

    def width_up_part(k):
        gather_wait_core(*va_gather, k)
        first = place(k)
        block = feat[0, :, pl.ds(pl.multiple_of(first // 2 * 640, 640), 640)]
        for pc in range(2):
            vectors = va[first + pc][:, :320]
            wacc[0] = wacc[0] + dot_nt(vectors, block[:, pc * 320:(pc + 1) * 320])

    def width_down_part(k):
        gather_wait_core(*vb_gather, k)
        first = place(k)
        block = feat[1, :, pl.ds(pl.multiple_of(first // 2 * 640, 640), 640)]
        for pc in range(2):
            vectors = jnp.concatenate([vb[first + pc], va[first + pc][:, 320:]], axis=1)
            wacc[1] = wacc[1] + dot_nt(vectors, block[:, pc * 320:(pc + 1) * 320])

    def scores_copy(k, pc):
        to = place(k) + pc
        return remote(acc.at[to], seq_in.at[s], seq_send.at[to], seq_recv.at[s], (to, b))

    def send_scores(k, pc):
        scores_copy(k, pc).start()

    def score(k, p, table):
        first = place(k)
        w = jnp.concatenate([table[first], table[first + 1]], axis=1).astype(F32)
        h = hid[k, :, pl.ds(p * 640, 640)]
        lines = []
        for q in range(6):
            spread = dot_nt(mult[p, q], h) * w
            lines.append(jnp.sum(jnp.sum(spread.reshape(40, 8, 256), axis=0), axis=0, keepdims=True))
        return jnp.concatenate(lines + [jnp.zeros((2, 256), F32)], axis=0)

    def score_up(k):
        half[k] = score(k, 0, wu)

    def score_down(k):
        first = place(k)
        flat = half[k] + score(k, 1, wd)
        acc[first] = flat[:, :128]
        acc[first + 1] = flat[:, 128:]
        send_scores(k, 1 - c)

        @pl.when(k > 0)
        def _():
            send_scores(k, c)

    wacc[...] = jnp.zeros_like(wacc)
    for n in (0, 1):
        loads[n].wait()
    gather_send(*x_gather, 0)
    gather_send(*va_gather, 0)
    for n in (2, 3):
        loads[n].wait()

    def at(i, offset, stage):
        @pl.when((i >= offset) & (i < offset + GROUPS))
        def _():
            stage(i - offset)

    def loop(low, high, stage):
        def body(k, _):
            stage(k)
            return 0

        lax.fori_loop(low, high, body, 0)

    def x_step(k):
        @pl.when(k > 0)
        def _():
            gather_step(*x_gather, k)

    def stepper(gather):
        return lambda k: gather_step(*gather, k)

    def twins(gather):
        return lambda k: gather_wait_core(*gather, k)

    def bounds(i, marks):
        low, high = marks[0][1], marks[0][1]
        for mark, value in marks[1:]:
            low = jnp.where(i > mark, value, low)
            high = jnp.where(i >= mark, value, high)
        return low, high

    def span_loop(i, marks, stage):
        low, high = bounds(i, marks)
        loop(low, high, stage)

    def run_width(i):
        @pl.when(i == VB_START)
        def _():
            gather_send(*vb_gather, 0)

        span_loop(i, VA_MARKS, stepper(va_gather))
        span_loop(i, VB_MARKS, stepper(vb_gather))
        span_loop(i, VAC_MARKS, width_up_part)
        span_loop(i, VBC_MARKS, width_down_part)

        @pl.when(i == WU_START)
        def _():
            wu[s] = wacc[0].astype(BF16)
            gather_send(*wu_gather, 0)

        @pl.when(i == WD_START)
        def _():
            wd[s] = wacc[1].astype(BF16)
            gather_send(*wd_gather, 0)

        span_loop(i, WU_MARKS, stepper(wu_gather))
        span_loop(i, WUC_MARKS, twins(wu_gather))
        span_loop(i, WD_MARKS, stepper(wd_gather))
        span_loop(i, WDC_MARKS, twins(wd_gather))

    def run_score(i):
        def done(n, start):
            return jnp.clip(jnp.minimum(n // 2 - O_ARRIVE + 1, RATE * (n - start + 1)), 0, GROUPS)

        loop(done(i - 1, SU_START), done(i, SU_START), score_up)
        loop(done(i - 1, SD_START), done(i, SD_START), score_down)

    def iteration(i, _):
        halves = 0
        for stage in ORDER:
            if stage == "a":
                at(i, O_X, x_step)
                at(i, O_PART, stage_partial)
            if stage == "b":
                at(i, O_NEAR, stage_near)
            if stage == "c":
                at(i, O_OWN, stage_own)
            if stage == "d":
                at(i, O_SUM, stage_sum)
            if stage == "e":
                at(i, O_SPREAD, stage_spread)
            if stage == "f":
                at(i, O_FORWARD, stage_forward)
            if stage == "g":
                at(i, O_ARRIVE, stage_arrive)
            if stage == "w":
                run_width(2 * i + halves)
            if stage == "s":
                run_score(2 * i + halves)
                halves += 1

        @pl.when(i == 0)
        def _():
            for n in (10, 11):
                loads[n].wait()

        return 0

    lax.fori_loop(0, O_ARRIVE + GROUPS, iteration, 0)

    seq_in[s] = acc[s]
    for d in range(1, N_SEQ):
        other = lax.rem(s + d, N_SEQ)
        remote(acc.at[other], seq_in.at[other], seq_send.at[other], seq_recv.at[other], (other, b)).wait_recv()
    seq_sum[...] = jnp.sum(seq_in[...], axis=0)

    def basis_copy(d, block):
        there = lax.rem(b + d, N_BASIS)
        block = there if block is None else block
        return remote(seq_sum, basis_in.at[block], basis_send.at[there], basis_recv.at[block], (s, there))

    for d in range(1, N_BASIS):
        basis_copy(d, b).start()
    basis_in[b] = seq_sum[...]
    for gather in (x_gather, va_gather, vb_gather, wu_gather, wd_gather):
        gather_drain(*gather)
    for d in range(1, N_SEQ):
        other = lax.rem(s + d, N_SEQ)
        remote(acc.at[other], seq_in.at[s], seq_send.at[other], seq_recv.at[s], (other, b)).wait_send()
    def drain(k, _):
        for n in range(18):
            h_copy(k, n).wait_send()
        return 0

    lax.fori_loop(0, GROUPS, drain, 0)
    for d in range(1, N_BASIS):
        basis_copy(d, None).wait_recv()
    out[...] = jnp.sum(basis_in[...], axis=0)[:6]
    for d in range(1, N_BASIS):
        basis_copy(d, b).wait_send()


def shards(*blocks):
    vmem = pltpu.VMEM
    blocks = blocks[:8] + tuple(jnp.swapaxes(block, -1, -2) for block in blocks[8:])
    return pl.pallas_call(
        kernel,
        out_shape=jax.ShapeDtypeStruct((6, 128), F32),
        in_specs=[pl.BlockSpec(memory_space=pl.ANY)] * 12,
        out_specs=pl.BlockSpec(memory_space=pltpu.VMEM),
        scratch_shapes=[
            vmem((16, 2, 128, 640), BF16),
            vmem((2, 640, 640), BF16),
            vmem((GROUPS, 256, 1280), BF16),
            vmem((GROUPS, 2, 32, 1280), BF16),
            vmem((GROUPS, 2, 64, 1280), BF16),
            vmem((GROUPS, 3, 16, 1280), BF16),
            vmem((GROUPS, 256, 1280), BF16),
            vmem((2, 320, 320), BF16),
            vmem((16, 320, 384), BF16),
            vmem((16, 320, 256), BF16),
            vmem((2, 128, 5120), BF16),
            vmem((2, 320, 128), F32),
            vmem((16, 320, 128), BF16),
            vmem((16, 320, 128), BF16),
            vmem((2, 6, 320, 640), BF16),
            vmem((2, 320, 640), F32),
            vmem((2, 6, 320, 640), BF16),
            vmem((GROUPS, 8, 256), F32),
            vmem((16, 8, 128), F32),
            vmem((16, 8, 128), F32),
            vmem((8, 128), F32),
            vmem((16, 8, 128), F32),
            pltpu.SemaphoreType.DMA((12,)),
            pltpu.SemaphoreType.DMA((4, GROUPS)),
            pltpu.SemaphoreType.DMA((16,)),
            pltpu.SemaphoreType.DMA((4, 4, GROUPS)),
            pltpu.SemaphoreType.DMA((4, 16)),
            pltpu.SemaphoreType.DMA((GROUPS, 18)),
            pltpu.SemaphoreType.DMA((GROUPS, 18)),
            pltpu.SemaphoreType.DMA((16,)),
            pltpu.SemaphoreType.DMA((16,)),
            pltpu.SemaphoreType.DMA((16,)),
            pltpu.SemaphoreType.DMA((16,)),
        ],
        compiler_params=pltpu.CompilerParams(
            collective_id=0, has_side_effects=True, vmem_limit_bytes=60 * 1024 * 1024
        ),
        cost_estimate=pl.CostEstimate(flops=14_000_000_000, bytes_accessed=12_000_000, transcendentals=0),
    )(*blocks)


def solution(mesh):
    return jax.shard_map(
        shards,
        mesh=mesh,
        in_specs=(
            P("seq", None),
            P("seq", "basis"),
            P("seq", "basis"),
            P("seq", None),
            P("basis", "seq"),
            P("basis", "seq"),
            P("seq", "basis"),
            P("seq", "basis"),
            P(None, "seq", "basis"),
            P(None, "seq", "basis"),
            P("seq", "basis"),
            P("seq", "basis"),
        ),
        out_specs=P(None, "seq"),
        check_vma=False,
    )
```

```python
import functools

import jax
import jax.numpy as jnp
from jax import lax
from jax.experimental import pallas as pl
from jax.experimental.pallas import tpu as pltpu
from jax.sharding import PartitionSpec as P

DAMPING = 0.1
MESH = pl.DeviceIdType.MESH
F32 = jnp.float32
BF16 = jnp.bfloat16

N_SEQ, N_BASIS = 16, 16
GROUPS = 8
ORDER = "gfedcbawsws"
O_X, O_PART, O_NEAR, O_OWN, O_SUM, O_SPREAD, O_FORWARD, O_ARRIVE = 0, 0, 1, 2, 3, 4, 5, 6
VB_START = 3
VA_MARKS = ((0, 1), (5, 2), (7, 4), (11, 6), (13, 8))
VB_MARKS = ((0, 1), (9, 2), (11, 4), (13, 6), (15, 8))
VAC_MARKS = ((0, 0), (7, 2), (9, 4), (13, 6), (15, 8))
VBC_MARKS = ((0, 0), (13, 2), (15, 6), (17, 8))
WU_START = 15
WU_MARKS = ((0, 1), (16, 2), (17, 6), (18, 8))
WUC_MARKS = ((0, 0), (18, 8))
WD_START = 17
WD_MARKS = ((0, 1), (18, 2), (19, 6), (20, 8))
WDC_MARKS = ((0, 0), (20, 8))
SU_START = 18
SD_START = 20
RATE = 2


def dot_nt(a, b):
    return lax.dot_general(a, b, (((1,), (1,)), ((), ())), preferred_element_type=F32)


def kernel(
    up_input, up_grad, down_input, down_grad, width_up, width_down, hidden_up, hidden_down,
    query_up, query_down, eigen_up, eigen_down,
    out,
    xg, vh, part, r1, r2, r3, hid, wide, va, vb, feat, wacc, wu, wd, query, eigen, mult,
    half, acc, seq_in, seq_sum, basis_in,
    local_sem, x_send, x_recv, g_send, g_recv,
    h_send, h_recv, seq_send, seq_recv, basis_send, basis_recv,
):
    s = lax.axis_index("seq")
    b = lax.axis_index("basis")
    x, zl, c = s // 4, lax.rem(s // 2, 2), lax.rem(s, 2)
    zh, y = b // 4, lax.rem(b, 4)
    x1, x2, x3 = lax.rem(x + 1, 4), lax.rem(x + 2, 4), lax.rem(x + 3, 4)
    y1, y2, y3 = lax.rem(y + 1, 4), lax.rem(y + 2, 4), lax.rem(y + 3, 4)

    def slot(px, pzl, pc):
        return px * 4 + pzl * 2 + pc

    def at_y(py):
        return (s, zh * 4 + py)

    def at_zh(d):
        return (s, lax.rem(zh + d, 4) * 4 + y)

    def at_x(px):
        return (slot(px, zl, c), b)

    to_core = (slot(x, zl, 1 - c), b)
    to_zl = (slot(x, 1 - zl, c), b)

    def remote(src, dst, send, recv, to):
        return pltpu.make_async_remote_copy(
            src_ref=src, dst_ref=dst, send_sem=send, recv_sem=recv, device_id=to, device_id_type=MESH
        )

    moves = [
        (up_grad, xg.at[s, 0]),
        (down_input, xg.at[s, 1]),
        (hidden_up, vh.at[0]),
        (hidden_down, vh.at[1]),
        (width_up, wide.at[0]),
        (width_down, wide.at[1]),
        (query_up, query.at[0]),
        (query_down, query.at[1]),
        (eigen_up, eigen.at[0]),
        (eigen_down, eigen.at[1]),
        (up_input, feat.at[0]),
        (down_grad, feat.at[1]),
    ]
    loads = [pltpu.make_async_copy(a, d, local_sem.at[n]) for n, (a, d) in enumerate(moves)]
    for load in loads:
        load.start()

    barrier = pltpu.get_barrier_semaphore()
    def prepare(p):
        def body(r, _):
            span = pl.ds(pl.multiple_of(r * 32, 32), 32)
            scale = 1.0 / (eigen[p, span, :] + DAMPING)
            for q in range(6):
                mult[p, q, span, :] = (query[p, q, span, :].astype(F32) * scale).astype(BF16)
            return 0

        lax.fori_loop(0, 10, body, 0)

    others = N_SEQ + N_BASIS - 2

    def along_seq(d):
        return (lax.rem(s + d, N_SEQ), b)

    def along_basis(d):
        return (s, lax.rem(b + d, N_BASIS))

    def greet(d, _):
        pl.semaphore_signal(barrier, inc=1, device_id=along_seq(d), device_id_type=MESH)
        pl.semaphore_signal(barrier, inc=1, device_id=along_basis(d), device_id_type=MESH)
        return 0

    lax.fori_loop(1, N_SEQ, greet, 0)
    for n in (6, 7, 8, 9):
        loads[n].wait()
    prepare(0)
    prepare(1)
    for n in (4, 5):
        loads[n].wait()
    va[s] = jnp.concatenate([wide[0], wide[1, :, 256:]], axis=1)
    vb[s] = wide[1, :, :256]
    pl.semaphore_wait(barrier, others)

    def place(k):
        px = jnp.where(k < 2, x, jnp.where(k >= 6, x2, jnp.where(lax.rem(k, 2) == 0, x3, x1)))
        own = (k == 0) | (k == 2) | (k == 3) | (k == 6)
        return px * 4 + jnp.where(own, zl, 1 - zl) * 2

    def gather_copy(buf, send, recv, k, way, to):
        block = buf.at[place(k) + c]
        return remote(block, block, send.at[way, k], recv.at[place(k) + c], to)

    def gather_send(buf, send, recv, k):
        gather_copy(buf, send, recv, k, 0, to_core).start()

        @pl.when(k == 0)
        def _():
            gather_copy(buf, send, recv, k, 1, to_zl).start()

        @pl.when(k <= 2)
        def _():
            gather_copy(buf, send, recv, k, 2, at_x(x1)).start()

        @pl.when((k <= 1) | (k == 5))
        def _():
            gather_copy(buf, send, recv, k, 3, at_x(x3)).start()

    def gather_wait(buf, send, recv, k):
        gather_copy(buf, send, recv, k, 0, to_core).wait_recv()

    def gather_wait_core(buf, send, recv, k):
        block = buf.at[place(k) + 1 - c]
        remote(block, block, send.at[0, k], recv.at[place(k) + 1 - c], to_core).wait_recv()

    def gather_step(buf, send, recv, k):
        @pl.when(k > 0)
        def _():
            gather_wait(buf, send, recv, k)

        gather_send(buf, send, recv, k)

    def gather_drain(buf, send, recv):
        def body(k, _):
            gather_copy(buf, send, recv, k, 0, to_core).wait_send()

            @pl.when(k == 0)
            def _():
                gather_copy(buf, send, recv, k, 1, to_zl).wait_send()

            @pl.when(k <= 2)
            def _():
                gather_copy(buf, send, recv, k, 2, at_x(x1)).wait_send()

            @pl.when((k <= 1) | (k == 5))
            def _():
                gather_copy(buf, send, recv, k, 3, at_x(x3)).wait_send()

            return 0

        lax.fori_loop(0, GROUPS, body, 0)

    x_gather = (xg, x_send, x_recv)
    va_gather = (va, g_send.at[0], g_recv.at[0])
    vb_gather = (vb, g_send.at[1], g_recv.at[1])
    wu_gather = (wu, g_send.at[2], g_recv.at[2])
    wd_gather = (wd, g_send.at[3], g_recv.at[3])

    def rows(py, first, count):
        return pl.ds(pl.multiple_of(py * 64 + first, 16), count)

    def h_copy(k, n):
        sems = (h_send.at[k, n], h_recv.at[k, n])
        if n == 0:
            return remote(part.at[k, rows(y2, 0, 32)], r1.at[k, 0], *sems, at_y(y1))
        if n == 1:
            return remote(part.at[k, rows(y2, 32, 32)], r1.at[k, 1], *sems, at_y(y3))
        if n == 2:
            return remote(part.at[k, rows(y1, 32, 32)], r2.at[k, 0, pl.ds(32, 32)], *sems, at_y(y1))
        if n == 3:
            return remote(part.at[k, rows(y3, 0, 32)], r2.at[k, 1, pl.ds(0, 32)], *sems, at_y(y3))
        if n == 4:
            return remote(part.at[k, rows(y1, 0, 32)], r2.at[k, 0, pl.ds(0, 32)], *sems, at_y(y1))
        if n == 5:
            return remote(part.at[k, rows(y3, 32, 32)], r2.at[k, 1, pl.ds(32, 32)], *sems, at_y(y3))
        if n < 9:
            d = n - 5
            piece = part.at[k, rows(y, lax.rem(zh + d, 4) * 16, 16)]
            return remote(piece, r3.at[k, d - 1], *sems, at_zh(d))
        if n < 12:
            d = n - 8
            piece = hid.at[k, rows(y, zh * 16, 16)]
            return remote(piece, piece, *sems, at_zh(d))
        if n == 12:
            piece, to = hid.at[k, rows(y, 0, 32)], at_y(y1)
        elif n == 13:
            piece, to = hid.at[k, rows(y, 32, 32)], at_y(y3)
        elif n == 14:
            piece, to = hid.at[k, rows(y, 32, 32)], at_y(y1)
        elif n == 15:
            piece, to = hid.at[k, rows(y, 0, 32)], at_y(y3)
        elif n == 16:
            piece, to = hid.at[k, rows(y3, 0, 32)], at_y(y1)
        else:
            piece, to = hid.at[k, rows(y1, 32, 32)], at_y(y3)
        return remote(piece, piece, *sems, to)

    def h_wait(k, n):
        if n == 0:
            dst = r1.at[k, 0]
        elif n == 1:
            dst = r1.at[k, 1]
        elif n in (2, 4):
            dst = r2.at[k, 0, pl.ds(32 if n == 2 else 0, 32)]
        elif n in (3, 5):
            dst = r2.at[k, 1, pl.ds(0 if n == 3 else 32, 32)]
        elif n < 9:
            dst = r3.at[k, n - 6]
        elif n < 12:
            dst = hid.at[k, rows(y, lax.rem(zh + 4 - (n - 8), 4) * 16, 16)]
        elif n == 12:
            dst = hid.at[k, rows(y3, 0, 32)]
        elif n == 13:
            dst = hid.at[k, rows(y1, 32, 32)]
        elif n == 14:
            dst = hid.at[k, rows(y3, 32, 32)]
        elif n == 15:
            dst = hid.at[k, rows(y1, 0, 32)]
        elif n == 16:
            dst = hid.at[k, rows(y2, 0, 32)]
        else:
            dst = hid.at[k, rows(y2, 32, 32)]
        remote(dst, dst, h_send.at[k, n], h_recv.at[k, n], at_y(y1)).wait_recv()

    def stage_partial(k):
        gather_wait_core(*x_gather, k)
        first = place(k)
        for p in range(2):
            rows_in = xg[pl.ds(first, 2), p].reshape(256, 640)
            part[k, :, pl.ds(p * 640, 640)] = dot_nt(rows_in, vh[p]).astype(BF16)
        for n in (0, 1, 2, 3):
            h_copy(k, n).start()

    def stage_near(k):
        h_wait(k, 0)
        span = rows(y1, 0, 32)
        part[k, span, :] = (part[k, span, :].astype(F32) + r1[k, 0].astype(F32)).astype(BF16)
        h_copy(k, 4).start()
        h_wait(k, 1)
        span = rows(y3, 32, 32)
        part[k, span, :] = (part[k, span, :].astype(F32) + r1[k, 1].astype(F32)).astype(BF16)
        h_copy(k, 5).start()

    def stage_own(k):
        for n in (2, 3, 4, 5):
            h_wait(k, n)
        span = rows(y, 0, 64)
        total = part[k, span, :].astype(F32) + r2[k, 0].astype(F32) + r2[k, 1].astype(F32)
        part[k, span, :] = total.astype(BF16)
        for n in (7, 6, 8):
            h_copy(k, n).start()

    def stage_sum(k):
        for n in (6, 7, 8):
            h_wait(k, n)
        span = rows(y, zh * 16, 16)
        total = part[k, span, :].astype(F32)
        for d in range(3):
            total = total + r3[k, d].astype(F32)
        hid[k, span, :] = total.astype(BF16)
        for n in (10, 9, 11):
            h_copy(k, n).start()

    def stage_spread(k):
        for n in (9, 10, 11):
            h_wait(k, n)
        for n in (12, 13, 14, 15):
            h_copy(k, n).start()

    def stage_forward(k):
        h_wait(k, 12)
        h_copy(k, 16).start()
        h_wait(k, 13)
        h_copy(k, 17).start()

    def stage_arrive(k):
        for n in (14, 15, 16, 17):
            h_wait(k, n)

    def width_up_part(k):
        gather_wait_core(*va_gather, k)
        first = place(k)
        block = feat[0, :, pl.ds(pl.multiple_of(first // 2 * 640, 640), 640)]
        for pc in range(2):
            vectors = va[first + pc][:, :320]
            wacc[0] = wacc[0] + dot_nt(vectors, block[:, pc * 320:(pc + 1) * 320])

    def width_down_part(k):
        gather_wait_core(*vb_gather, k)
        first = place(k)
        block = feat[1, :, pl.ds(pl.multiple_of(first // 2 * 640, 640), 640)]
        for pc in range(2):
            vectors = jnp.concatenate([vb[first + pc], va[first + pc][:, 320:]], axis=1)
            wacc[1] = wacc[1] + dot_nt(vectors, block[:, pc * 320:(pc + 1) * 320])

    def scores_copy(k, pc):
        to = place(k) + pc
        return remote(acc.at[to], seq_in.at[s], seq_send.at[to], seq_recv.at[s], (to, b))

    def send_scores(k, pc):
        scores_copy(k, pc).start()

    def score(k, p, table):
        first = place(k)
        w = jnp.concatenate([table[first], table[first + 1]], axis=1).astype(F32)
        h = hid[k, :, pl.ds(p * 640, 640)]
        lines = []
        for q in range(6):
            spread = dot_nt(mult[p, q], h) * w
            lines.append(jnp.sum(jnp.sum(spread.reshape(40, 8, 256), axis=0), axis=0, keepdims=True))
        return jnp.concatenate(lines + [jnp.zeros((2, 256), F32)], axis=0)

    def score_up(k):
        half[k] = score(k, 0, wu)

    def score_down(k):
        first = place(k)
        flat = half[k] + score(k, 1, wd)
        acc[first] = flat[:, :128]
        acc[first + 1] = flat[:, 128:]
        send_scores(k, 1 - c)

        @pl.when(k > 0)
        def _():
            send_scores(k, c)

    wacc[...] = jnp.zeros_like(wacc)
    for n in (0, 1):
        loads[n].wait()
    gather_send(*x_gather, 0)
    gather_send(*va_gather, 0)
    for n in (2, 3):
        loads[n].wait()

    def at(i, offset, stage):
        @pl.when((i >= offset) & (i < offset + GROUPS))
        def _():
            stage(i - offset)

    def loop(low, high, stage):
        def body(k, _):
            stage(k)
            return 0

        lax.fori_loop(low, high, body, 0)

    def x_step(k):
        @pl.when(k > 0)
        def _():
            gather_step(*x_gather, k)

    def stepper(gather):
        return lambda k: gather_step(*gather, k)

    def twins(gather):
        return lambda k: gather_wait_core(*gather, k)

    def bounds(i, marks):
        low, high = marks[0][1], marks[0][1]
        for mark, value in marks[1:]:
            low = jnp.where(i > mark, value, low)
            high = jnp.where(i >= mark, value, high)
        return low, high

    def span_loop(i, marks, stage):
        low, high = bounds(i, marks)
        loop(low, high, stage)

    def run_width(i):
        @pl.when(i == VB_START)
        def _():
            gather_send(*vb_gather, 0)

        span_loop(i, VA_MARKS, stepper(va_gather))
        span_loop(i, VB_MARKS, stepper(vb_gather))
        span_loop(i, VAC_MARKS, width_up_part)
        span_loop(i, VBC_MARKS, width_down_part)

        @pl.when(i == WU_START)
        def _():
            wu[s] = wacc[0].astype(BF16)
            gather_send(*wu_gather, 0)

        @pl.when(i == WD_START)
        def _():
            wd[s] = wacc[1].astype(BF16)
            gather_send(*wd_gather, 0)

        span_loop(i, WU_MARKS, stepper(wu_gather))
        span_loop(i, WUC_MARKS, twins(wu_gather))
        span_loop(i, WD_MARKS, stepper(wd_gather))
        span_loop(i, WDC_MARKS, twins(wd_gather))

    def run_score(i):
        def done(n, start):
            return jnp.clip(jnp.minimum(n // 2 - O_ARRIVE + 1, RATE * (n - start + 1)), 0, GROUPS)

        loop(done(i - 1, SU_START), done(i, SU_START), score_up)
        loop(done(i - 1, SD_START), done(i, SD_START), score_down)

    def iteration(i, _):
        halves = 0
        for stage in ORDER:
            if stage == "a":
                at(i, O_X, x_step)
                at(i, O_PART, stage_partial)
            if stage == "b":
                at(i, O_NEAR, stage_near)
            if stage == "c":
                at(i, O_OWN, stage_own)
            if stage == "d":
                at(i, O_SUM, stage_sum)
            if stage == "e":
                at(i, O_SPREAD, stage_spread)
            if stage == "f":
                at(i, O_FORWARD, stage_forward)
            if stage == "g":
                at(i, O_ARRIVE, stage_arrive)
            if stage == "w":
                run_width(2 * i + halves)
            if stage == "s":
                run_score(2 * i + halves)
                halves += 1

        @pl.when(i == 0)
        def _():
            for n in (10, 11):
                loads[n].wait()

        return 0

    lax.fori_loop(0, O_ARRIVE + GROUPS, iteration, 0)

    seq_in[s] = acc[s]
    for d in range(1, N_SEQ):
        other = lax.rem(s + d, N_SEQ)
        remote(acc.at[other], seq_in.at[other], seq_send.at[other], seq_recv.at[other], (other, b)).wait_recv()
    seq_sum[...] = jnp.sum(seq_in[...], axis=0)

    def basis_copy(d, block):
        there = lax.rem(b + d, N_BASIS)
        block = there if block is None else block
        return remote(seq_sum, basis_in.at[block], basis_send.at[there], basis_recv.at[block], (s, there))

    for d in range(1, N_BASIS):
        basis_copy(d, b).start()
    basis_in[b] = seq_sum[...]
    for gather in (x_gather, va_gather, vb_gather, wu_gather, wd_gather):
        gather_drain(*gather)
    for d in range(1, N_SEQ):
        other = lax.rem(s + d, N_SEQ)
        remote(acc.at[other], seq_in.at[s], seq_send.at[other], seq_recv.at[s], (other, b)).wait_send()
    def drain(k, _):
        for n in range(18):
            h_copy(k, n).wait_send()
        return 0

    lax.fori_loop(0, GROUPS, drain, 0)
    for d in range(1, N_BASIS):
        basis_copy(d, None).wait_recv()
    out[...] = jnp.sum(basis_in[...], axis=0)[:6]
    for d in range(1, N_BASIS):
        basis_copy(d, b).wait_send()


def shards(*blocks):
    vmem = pltpu.VMEM
    blocks = blocks[:8] + tuple(jnp.swapaxes(block, -1, -2) for block in blocks[8:])
    return pl.pallas_call(
        kernel,
        out_shape=jax.ShapeDtypeStruct((6, 128), F32),
        in_specs=[pl.BlockSpec(memory_space=pl.ANY)] * 12,
        out_specs=pl.BlockSpec(memory_space=pltpu.VMEM),
        scratch_shapes=[
            vmem((16, 2, 128, 640), BF16),
            vmem((2, 640, 640), BF16),
            vmem((GROUPS, 256, 1280), BF16),
            vmem((GROUPS, 2, 32, 1280), BF16),
            vmem((GROUPS, 2, 64, 1280), BF16),
            vmem((GROUPS, 3, 16, 1280), BF16),
            vmem((GROUPS, 256, 1280), BF16),
            vmem((2, 320, 320), BF16),
            vmem((16, 320, 384), BF16),
            vmem((16, 320, 256), BF16),
            vmem((2, 128, 5120), BF16),
            vmem((2, 320, 128), F32),
            vmem((16, 320, 128), BF16),
            vmem((16, 320, 128), BF16),
            vmem((2, 6, 320, 640), BF16),
            vmem((2, 320, 640), F32),
            vmem((2, 6, 320, 640), BF16),
            vmem((GROUPS, 8, 256), F32),
            vmem((16, 8, 128), F32),
            vmem((16, 8, 128), F32),
            vmem((8, 128), F32),
            vmem((16, 8, 128), F32),
            pltpu.SemaphoreType.DMA((12,)),
            pltpu.SemaphoreType.DMA((4, GROUPS)),
            pltpu.SemaphoreType.DMA((16,)),
            pltpu.SemaphoreType.DMA((4, 4, GROUPS)),
            pltpu.SemaphoreType.DMA((4, 16)),
            pltpu.SemaphoreType.DMA((GROUPS, 18)),
            pltpu.SemaphoreType.DMA((GROUPS, 18)),
            pltpu.SemaphoreType.DMA((16,)),
            pltpu.SemaphoreType.DMA((16,)),
            pltpu.SemaphoreType.DMA((16,)),
            pltpu.SemaphoreType.DMA((16,)),
        ],
        compiler_params=pltpu.CompilerParams(
            collective_id=0, has_side_effects=True, vmem_limit_bytes=60 * 1024 * 1024
        ),
        cost_estimate=pl.CostEstimate(flops=14_000_000_000, bytes_accessed=12_000_000, transcendentals=0),
    )(*blocks)


def solution(mesh):
    return jax.shard_map(
        shards,
        mesh=mesh,
        in_specs=(
            P("seq", None),
            P("seq", "basis"),
            P("seq", "basis"),
            P("seq", None),
            P("basis", "seq"),
            P("basis", "seq"),
            P("seq", "basis"),
            P("seq", "basis"),
            P(None, "seq", "basis"),
            P(None, "seq", "basis"),
            P("seq", "basis"),
            P("seq", "basis"),
        ),
        out_specs=P(None, "seq"),
        check_vma=False,
    )
```
